1024 devices in a mesh: dp: 128 (over x, y, core), tensor: 8 (over z).
Axes of the slice: x: 8, y: 8, z: 8, core: 2. Of those that a mesh axis runs over, the one named last changes fastest.
Arguments:
- tokens: bfloat16 [16384, 8192], P('dp', 'tensor'), may hold values from -6 to 6
- kv_weight: bfloat16 [8192, 2048], P('tensor'), may hold values from -0.0625 to 0.0625
- adapter_down: bfloat16 [512, 8, 1024, 32], P(None, 'tensor', 'dp'), may hold values from -0.0625 to 0.0625
- adapter_up: bfloat16 [512, 32, 8, 256], P(None, None, 'tensor', 'dp'), may hold values from -1 to 1
- cotangent: bfloat16 [16384, 2048], P('dp'), may hold values from -1.5 to 1.5
- block_adapter: int32 [128], replicated, may hold values from 0 to 511
- block_rows: int32 [128], P('dp'), may hold values from 32 to 128
Outputs:
- key_value_output: bfloat16 [16384, 2048], P('dp', 'tensor')
- token_gradient: bfloat16 [16384, 8192], P('dp', 'tensor')
- grad_down: float32 [512, 8, 1024, 32], P(None, 'tensor', 'dp')
- grad_up: float32 [512, 32, 8, 256], P(None, None, 'tensor', 'dp')
The draws below stay inside these ranges and needn't reach their ends.
Inputs may be any that keep to these rules, and one draw needn't show every extreme that they name: `block_adapter`: block j belongs to the tokens of dp index j; an adapter may serve many blocks or none. `block_rows`: the live rows of a block come first.
All inputs are finite; a program needn't handle non-finite values.
Results may differ from the reference program's by a relative error of at most 0.015.
Values may be sent and summed in bfloat16 or wider, within the bound.
A program may use at most 32 MiB of HBM per device.

```python
import math
import jax
import jax.numpy as jnp
import numpy as np
from jax import lax

D = 8192
KV = 2048
R = 32
BLK = 128
BLOCKS = 128
TOKENS = 16384
ADAPTERS = 512
TSPLIT = 8
DT = 1024
KT = 256


def with_ends(drawn, own_key, least, largest):
    extent = drawn.shape
    place = [jax.random.randint(jax.random.fold_in(own_key, axis), (), 0, extent[axis]) for axis in range(len(extent))]
    drawn = drawn.at[tuple(place)].set(least)
    longest = extent.index(max(extent))
    place[longest] = (place[longest] + 1) % extent[longest]
    return drawn.at[tuple(place)].set(largest)


def shard_levels(own_key, dims, shards, low, top_value):
    gain = 1.0
    for position, blocks in shards:
        steps = jax.random.uniform(jax.random.fold_in(jax.random.fold_in(own_key, 6), position), (blocks,), jnp.float32, low / len(shards), top_value / len(shards))
        gain = gain * jnp.repeat(jnp.exp(steps), dims[position] // blocks).reshape((-1,) + (1,) * (len(dims) - 1 - position))
    return gain


def rank_table(amount, lean):
    portions = [(1 << 20) // math.isqrt(grade ** lean) + 1 for grade in range(1, amount + 1)]
    deviation = 1 + sum(portions) // (1 << 30)
    return np.cumsum(np.array([max(1, weight // deviation) for weight in portions]))


def skewed_ids(key, dims, number_of, lean):
    table = rank_table(number_of, lean)
    pick = jax.random.randint(jax.random.fold_in(key, 1), dims, 0, int(table[number_of - 1]))
    standing = jnp.searchsorted(jnp.asarray(table, jnp.int32), pick, side="right")
    return jax.random.permutation(jax.random.fold_in(key, 2), number_of)[standing].astype(jnp.int32)


def noise(key, shape, scale, limit, cuts=(), held_as=jnp.bfloat16):
    level = shard_levels(key, shape, cuts, -0.22, 0.18) if cuts else 1.0
    values = jax.random.normal(key, shape, jnp.float32) * scale * level
    return jnp.minimum(jnp.maximum(values, -limit), limit).astype(held_as)


def setup_inputs(seed: int = 0) -> dict:
    arg_keys = jax.random.split(jax.random.key(seed), 8)
    tokens = noise(arg_keys[0], (TOKENS, D), 1.0, 6.0, ((0, 128), (1, 8)))
    kv_weight = noise(arg_keys[1], (D, KV), D ** -0.5, 0.0625, ((0, 8),))
    adapter_down = noise(arg_keys[2], (ADAPTERS, TSPLIT, DT, R), D ** -0.5, 0.0625, ((1, 8), (2, 128)))
    adapter_up = noise(arg_keys[3], (ADAPTERS, R, TSPLIT, KT), R ** -0.5, 1.0, ((2, 8), (3, 128)))
    cotangent = noise(arg_keys[4], (TOKENS, KV), 0.25, 1.5, ((0, 128),))
    block_adapter = with_ends(skewed_ids(arg_keys[5], (BLOCKS,), ADAPTERS, 2), jax.random.fold_in(arg_keys[5], 3), 0, ADAPTERS - 1).astype(jnp.int32)
    block_rows = with_ends(jax.random.randint(arg_keys[6], (BLOCKS,), BLK // 4, BLK + 1), jax.random.fold_in(arg_keys[6], 1), BLK // 4, BLK).astype(jnp.int32)
    return {"tokens": tokens, "kv_weight": kv_weight, "adapter_down": adapter_down, "adapter_up": adapter_up, "cotangent": cotangent, "block_adapter": block_adapter, "block_rows": block_rows}


def reference(tokens, kv_weight, adapter_down, adapter_up, cotangent, block_adapter, block_rows):
    down_all = adapter_down.reshape(ADAPTERS, D, R)
    up_all = adapter_up.reshape(ADAPTERS, R, KV)
    live_rows = jnp.arange(BLK, dtype=jnp.int32)[None, :] < block_rows[:, None]
    row_selection_mask = live_rows.astype(jnp.bfloat16)
    tok_blocks = tokens.reshape(BLOCKS, BLK, D)
    dy_blocks = (cotangent.reshape(BLOCKS, BLK, KV) * row_selection_mask[:, :, None]).astype(jnp.bfloat16)

    def per_block(items):
        tok_rows, dy_rows, masked_rows, adapter_id = items
        down_projection = down_all[adapter_id]
        up_projection = up_all[adapter_id]
        rank_activation = jnp.dot(tok_rows, down_projection, preferred_element_type=jnp.float32).astype(jnp.bfloat16)
        rank_gradient = jnp.dot(dy_rows, up_projection.T, preferred_element_type=jnp.float32).astype(jnp.bfloat16)
        frozen_output = jnp.dot(tok_rows, kv_weight, preferred_element_type=jnp.float32)
        adapter_output = jnp.dot(rank_activation, up_projection, preferred_element_type=jnp.float32)
        output_rows = ((frozen_output + adapter_output) * masked_rows[:, None].astype(jnp.float32)).astype(jnp.bfloat16)
        backward_frozen_term = jnp.dot(dy_rows, kv_weight.T, preferred_element_type=jnp.float32)
        backward_adapter_term = jnp.dot(rank_gradient, down_projection.T, preferred_element_type=jnp.float32)
        gradient_rows = (backward_frozen_term + backward_adapter_term).astype(jnp.bfloat16)
        down_term = jnp.dot(tok_rows.T, rank_gradient, preferred_element_type=jnp.float32).astype(jnp.bfloat16)
        up_term = jnp.dot(rank_activation.T, dy_rows, preferred_element_type=jnp.float32).astype(jnp.bfloat16)
        return output_rows, gradient_rows, down_term, up_term

    output_rows, gradient_rows, down_terms, up_terms = lax.map(per_block, (tok_blocks, dy_blocks, row_selection_mask, block_adapter))
    key_value_output = output_rows.reshape(TOKENS, KV)
    token_gradient = gradient_rows.reshape(TOKENS, D)
    grad_down = jax.ops.segment_sum(down_terms.astype(jnp.float32), block_adapter, num_segments=ADAPTERS)
    grad_up = jax.ops.segment_sum(up_terms.astype(jnp.float32), block_adapter, num_segments=ADAPTERS)
    grad_down = grad_down.reshape(ADAPTERS, TSPLIT, DT, R)
    grad_up = grad_up.reshape(ADAPTERS, R, TSPLIT, KT)
    return key_value_output, token_gradient, grad_down, grad_up
```

```python
import jax
import jax.numpy as jnp
from jax import lax
from jax.experimental import pallas as pl
from jax.experimental.pallas import tpu as pltpu
from jax.sharding import PartitionSpec as P

MESH = pl.DeviceIdType.MESH
BF16 = jnp.bfloat16
F32 = jnp.float32
X, Y, CORES, Z = 8, 8, 2, 8
GROUPS = X * Y * CORES
LANES = 128
NEAR = (1, 7, 2, 6)
FAR = (3, 5, 4)


def ring(step, size):
    return min(step, size - step)


OFFSETS = sorted(
    [(x, y, c) for x in range(X) for y in range(Y) for c in range(CORES) if (x, y, c) != (0, 0, 0)],
    key=lambda o: -(ring(o[0], X) + ring(o[1], Y)),
)


def nn(a, b):
    return lax.dot_general(a, b, (((1,), (0,)), ((), ())), preferred_element_type=F32)


def nt(a, b):
    return lax.dot_general(a, b, (((1,), (1,)), ((), ())), preferred_element_type=F32)


def kernel(
    rows_ref, tok_hbm, w_hbm, down_hbm, up_hbm, cot_hbm, ids_hbm,
    kv_hbm, tg_hbm, gd_hbm, gu_hbm,
    tok, w, down, up, dy, ids,
    pick, send1, recv1, send2, recv2, part, parts, chunk, chunks,
    tok_perm, tok_cols, dy_cols, dy_cols_t, frozen, back, m_down,
    kv, tg, gd, gu,
    in_sem, own_sem, a_send, a_recv, p_send, p_recv, c_send, c_recv, g_send, g_recv, out_sem,
):
    n, features = tok.shape
    rank = 32
    cols = kv.shape[1]
    adapters = down.shape[1]
    me = lax.axis_index("dp")
    col = lax.axis_index("tensor")
    mx, my, mc = me // (Y * CORES), (me // CORES) % Y, me % CORES

    loads = [
        pltpu.make_async_copy(src, dst, in_sem.at[i])
        for i, (src, dst) in enumerate(
            [(ids_hbm, ids), (down_hbm, down), (up_hbm, up), (tok_hbm, tok), (cot_hbm, dy), (w_hbm, w)]
        )
    ]
    for load in loads:
        load.start()

    def group_peer(o):
        return ((mx + o[0]) % X) * (Y * CORES) + ((my + o[1]) % Y) * CORES + (mc + o[2]) % CORES

    barrier = pltpu.get_barrier_semaphore()
    for o in OFFSETS:
        pl.semaphore_signal(barrier, inc=1, device_id=(group_peer(o), col), device_id_type=MESH)
    for i in (4, 3, 5, 2, 6, 1, 7):
        pl.semaphore_signal(barrier, inc=1, device_id=(me, (col + i) % Z), device_id_type=MESH)

    loads[0].wait()
    pairs = 2 * GROUPS
    at = lax.broadcasted_iota(jnp.int32, (pairs, GROUPS), 0) // 2
    lane = lax.broadcasted_iota(jnp.int32, (pairs, GROUPS), 1)
    own = jnp.sum(jnp.where(at == lane, ids[...].astype(F32), 0.0), axis=1, keepdims=True)
    row = lax.broadcasted_iota(jnp.int32, (pairs, adapters), 0)
    hit = lax.broadcasted_iota(jnp.int32, (pairs, adapters), 1).astype(F32) == own
    for h in range(2):
        pick[:, h * adapters:(h + 1) * adapters] = jnp.where(hit & (row % 2 == h), 1.0, 0.0).astype(BF16)
    even, odd = pick[:, :adapters], pick[:, adapters:]

    loads[1].wait()
    down_rows = nt(even, down[:LANES]) + nt(odd, down[LANES:])
    send1[0] = down_rows.astype(BF16).reshape(GROUPS, 2, LANES)
    loads[2].wait()
    up_wide = up[...].astype(F32)
    up_rows = nt(even, up_wide[:, 0, :].astype(BF16)) + nt(odd, up_wide[:, 1, :].astype(BF16))
    pad = jnp.zeros((pairs, LANES - rank), F32)
    send1[1] = jnp.concatenate([up_rows, pad], axis=1).astype(BF16).reshape(GROUPS, 2, LANES)

    pl.semaphore_wait(barrier, len(OFFSETS) + Z - 1)

    def exchange(src, dst, send_sem, recv_sem, local_sem):
        for o in OFFSETS:
            peer = group_peer(o)
            pltpu.make_async_remote_copy(
                src.at[:, peer], dst.at[:, me], send_sem, recv_sem,
                device_id=(peer, col), device_id_type=MESH,
            ).start()
        local = pltpu.make_async_copy(src.at[:, me], dst.at[:, me], local_sem)
        local.start()
        every = pltpu.make_async_remote_copy(
            src.at[:, 0:GROUPS - 1], dst.at[:, 0:GROUPS - 1], send_sem, recv_sem,
            device_id=(me, (col + 1) % Z), device_id_type=MESH,
        )
        return local, every

    local1, every1 = exchange(send1, recv1, a_send, a_recv, own_sem.at[0])

    loads[3].wait()
    loads[5].wait()

    def frozen_part(i):
        to = (col + i) % Z
        start = pl.multiple_of(to * cols, cols)
        return to, nn(tok[...], w[:, pl.ds(start, cols)])

    def send_chunk(i):
        to, value = frozen_part(i)
        chunk[i] = value.astype(BF16)
        pltpu.make_async_remote_copy(
            chunk.at[i], chunks.at[col], c_send, c_recv, device_id=(me, to), device_id_type=MESH
        ).start()

    for i in NEAR:
        send_chunk(i)

    i0 = lax.broadcasted_iota(jnp.int32, (LANES, LANES), 0)
    i1 = lax.broadcasted_iota(jnp.int32, (LANES, LANES), 1)
    order = jnp.where(i1 == (i0 % 32) * 4 + i0 // 32, 1.0, 0.0).astype(BF16)
    order_t = jnp.where(i0 == (i1 % 32) * 4 + i1 // 32, 1.0, 0.0).astype(BF16)
    blocks = features // LANES
    for k in range(blocks):
        span = slice(k * LANES, (k + 1) * LANES)
        tok_perm[:, span] = nt(tok[:, span], order).astype(BF16)
        turned = nt(order, tok[:, span]).astype(BF16)
        for j in range(4):
            tok_cols[k * 32:(k + 1) * 32, j * n:(j + 1) * n] = turned[j * 32:(j + 1) * 32]

    loads[4].wait()
    live = lax.broadcasted_iota(jnp.int32, (n, 1), 0) < rows_ref[0]
    mask = jnp.where(live, 1.0, 0.0)
    dy[...] = dy[...] * mask.astype(BF16)
    mine = pl.multiple_of(col * cols, cols)
    dy_cols[...] = dy[:, pl.ds(mine, cols)]
    dy_cols_t[...] = dy_cols[...].T
    frozen[...] = frozen_part(0)[1]

    local1.wait()
    every1.wait_recv()
    a_mat = recv1[0].reshape(pairs, LANES)
    b_mat = recv1[1].reshape(pairs, LANES)[:, :rank]
    a_tall = jnp.concatenate(
        [a_mat[k * 32:(k + 1) * 32, j * rank:(j + 1) * rank] for k in range(blocks) for j in range(4)], axis=0
    )
    sums = jnp.concatenate([nn(tok_perm[...], a_tall), nn(dy_cols[...], b_mat)], axis=1)
    half = n // 2
    part[...] = jnp.concatenate([sums[:half], sums[half:]], axis=1).astype(BF16)
    for i in (4, 3, 5, 2, 6, 1, 7):
        pltpu.make_async_remote_copy(
            part, parts.at[col], p_send, p_recv, device_id=(me, (col + i) % Z), device_id_type=MESH
        ).start()
    parts[col] = part[...]

    for i in FAR:
        send_chunk(i)
    for k in range(blocks):
        span = slice(k * LANES, (k + 1) * LANES)
        m_down[span] = nn(order_t, a_tall[span]).astype(BF16)
    wide = 256
    for k in range(features // wide):
        back[:, k * wide:(k + 1) * wide] = nt(dy[...], w[k * wide:(k + 1) * wide, :])

    every_part = pltpu.make_async_remote_copy(
        parts.at[0:Z - 1], parts.at[0:Z - 1], p_send, p_recv,
        device_id=(me, (col + 1) % Z), device_id_type=MESH,
    )
    every_part.wait_recv()
    total = parts[0].astype(F32)
    for i in range(1, Z):
        total = total + parts[i].astype(F32)
    total = total.astype(BF16)
    act = jnp.concatenate([total[:, :rank], total[:, 2 * rank:3 * rank]], axis=0)
    grad = jnp.concatenate([total[:, rank:2 * rank], total[:, 3 * rank:]], axis=0)

    grad4 = jnp.concatenate([grad] * 4, axis=1)
    place = lax.broadcasted_iota(jnp.int32, (n, LANES), 1) // rank
    spread = jnp.concatenate(
        [jnp.where(place == j, grad4, jnp.zeros_like(grad4)) for j in range(4)], axis=0
    )
    send2[0] = nn(tok_cols[...], spread).astype(BF16).reshape(GROUPS, 2, LANES)
    up_term = nn(dy_cols_t[...], act)
    send2[1] = jnp.concatenate([up_term, pad], axis=1).astype(BF16).reshape(GROUPS, 2, LANES)
    local2, every2 = exchange(send2, recv2, g_send, g_recv, own_sem.at[1])

    tg[...] = (back[...] + nt(grad, m_down[...])).astype(BF16)
    out_tg = pltpu.make_async_copy(tg, tg_hbm, out_sem.at[0])
    out_tg.start()
    every_chunk = pltpu.make_async_remote_copy(
        chunk.at[1:Z], chunks.at[0:Z - 1], c_send, c_recv,
        device_id=(me, (col + 1) % Z), device_id_type=MESH,
    )
    every_chunk.wait_recv()
    chunks[col] = jnp.zeros((n, cols), BF16)
    kv_sum = frozen[...] + nt(act, b_mat)
    for i in range(Z):
        kv_sum = kv_sum + chunks[i].astype(F32)
    kv[...] = (kv_sum * mask).astype(BF16)
    out_kv = pltpu.make_async_copy(kv, kv_hbm, out_sem.at[1])
    out_kv.start()
    every1.wait_send()
    every_part.wait_send()
    every_chunk.wait_send()

    local2.wait()
    every2.wait_recv()
    terms = jnp.concatenate(
        [recv2[0].reshape(pairs, LANES).T, recv2[1].reshape(pairs, LANES).T[:rank]], axis=0
    )
    for h in range(2):
        sums = nn(terms, pick[:, h * adapters:(h + 1) * adapters])
        gd[h * LANES:(h + 1) * LANES] = sums[:LANES]
        gu[:, h, :] = sums[LANES:]
    out_gd = pltpu.make_async_copy(gd, gd_hbm, out_sem.at[2])
    out_gu = pltpu.make_async_copy(gu, gu_hbm, out_sem.at[3])
    out_gd.start()
    out_gu.start()
    every2.wait_send()
    out_tg.wait()
    out_kv.wait()
    out_gd.wait()
    out_gu.wait()


def shards(tokens, kv_weight, adapter_down, adapter_up, cotangent, block_adapter, block_rows):
    n, features = tokens.shape
    kv_width = kv_weight.shape[1]
    adapters, _, slice_rows, rank = adapter_down.shape
    slice_cols = adapter_up.shape[3]
    cols = kv_width // Z
    down_table = adapter_down.transpose(1, 2, 3, 0).reshape(slice_rows * rank, adapters)
    up_table = adapter_up.transpose(2, 1, 3, 0).reshape(rank, slice_cols, adapters)
    ids = block_adapter.reshape(1, GROUPS)
    pairs = 2 * GROUPS
    vmem, dma = pltpu.VMEM, pltpu.SemaphoreType.DMA
    any_spec = pl.BlockSpec(memory_space=pl.ANY)
    kv, tg, gd, gu = pl.pallas_call(
        kernel,
        out_shape=[
            jax.ShapeDtypeStruct((n, cols), BF16),
            jax.ShapeDtypeStruct((n, features), BF16),
            jax.ShapeDtypeStruct((slice_rows * rank, adapters), F32),
            jax.ShapeDtypeStruct((rank, slice_cols, adapters), F32),
        ],
        in_specs=[pl.BlockSpec(memory_space=pltpu.SMEM)] + [any_spec] * 6,
        out_specs=[any_spec] * 4,
        scratch_shapes=[
            vmem((n, features), BF16),
            vmem((features, kv_width), BF16),
            vmem((slice_rows * rank, adapters), BF16),
            vmem((rank, slice_cols, adapters), BF16),
            vmem((n, kv_width), BF16),
            vmem((1, GROUPS), jnp.int32),
            vmem((pairs, 2 * adapters), BF16),
            vmem((2, GROUPS, 2, LANES), BF16),
            vmem((2, GROUPS, 2, LANES), BF16),
            vmem((2, GROUPS, 2, LANES), BF16),
            vmem((2, GROUPS, 2, LANES), BF16),
            vmem((n // 2, 4 * rank), BF16),
            vmem((Z, n // 2, 4 * rank), BF16),
            vmem((Z, n, cols), BF16),
            vmem((Z, n, cols), BF16),
            vmem((n, features), BF16),
            vmem((pairs, 4 * n), BF16),
            vmem((n, cols), BF16),
            vmem((cols, n), BF16),
            vmem((n, cols), F32),
            vmem((n, features), F32),
            vmem((features, rank), BF16),
            vmem((n, cols), BF16),
            vmem((n, features), BF16),
            vmem((slice_rows * rank, adapters), F32),
            vmem((rank, slice_cols, adapters), F32),
            dma((6,)),
            dma((2,)),
            dma, dma, dma, dma, dma, dma, dma, dma,
            dma((4,)),
        ],
        compiler_params=pltpu.CompilerParams(
            collective_id=0, has_side_effects=True, vmem_limit_bytes=40 << 20
        ),
        name="fused",
    )(block_rows, tokens, kv_weight, down_table, up_table, cotangent, ids)
    grad_down = gd.reshape(1, slice_rows, rank, adapters).transpose(3, 0, 1, 2)
    grad_up = gu.reshape(1, rank, slice_cols, adapters).transpose(3, 1, 0, 2)
    return kv, tg, grad_down, grad_up


def solution(mesh):
    return jax.shard_map(
        shards,
        mesh=mesh,
        in_specs=(
            P("dp", "tensor"),
            P("tensor", None),
            P(None, "tensor", "dp", None),
            P(None, None, "tensor", "dp"),
            P("dp", None),
            P(),
            P("dp"),
        ),
        out_specs=(
            P("dp", "tensor"),
            P("dp", "tensor"),
            P(None, "tensor", "dp", None),
            P(None, None, "tensor", "dp"),
        ),
        check_vma=False,
    )
```

```python
import jax
import jax.numpy as jnp
from jax import lax
from jax.experimental import pallas as pl
from jax.experimental.pallas import tpu as pltpu
from jax.sharding import PartitionSpec as P

MESH = pl.DeviceIdType.MESH
BF16 = jnp.bfloat16
F32 = jnp.float32
X, Y, CORES, Z = 8, 8, 2, 8
GROUPS = X * Y * CORES
LANES = 128
NEAR = (1, 7, 2, 6)
FAR = (3, 5, 4)


def ring(step, size):
    return min(step, size - step)


OFFSETS = sorted(
    [(x, y, c) for x in range(X) for y in range(Y) for c in range(CORES) if (x, y, c) != (0, 0, 0)],
    key=lambda o: -(ring(o[0], X) + ring(o[1], Y)),
)
GREETINGS = sorted(
    OFFSETS + list(range(1, Z)),
    key=lambda o: -ring(o, Z) if isinstance(o, int) else -(ring(o[0], X) + ring(o[1], Y)),
)


def nn(a, b):
    return lax.dot_general(a, b, (((1,), (0,)), ((), ())), preferred_element_type=F32)


def nt(a, b):
    return lax.dot_general(a, b, (((1,), (1,)), ((), ())), preferred_element_type=F32)


def kernel(
    rows_ref, tok_hbm, w_hbm, down_hbm, up_hbm, cot_hbm, ids_hbm,
    kv, tg, recv2, pick,
    tok, w, down, up, dy, ids,
    send1, recv1, send2, part, parts, chunk, chunks,
    tok_perm, tok_cols, dy_cols, dy_cols_t, frozen, back, m_down,
    in_sem, own_sem, a_send, a_recv, p_send, p_recv, c_send, c_recv, g_send, g_recv,
):
    n, features = tok.shape
    rank = 32
    cols = kv.shape[1]
    adapters = down.shape[1]
    me = lax.axis_index("dp")
    col = lax.axis_index("tensor")
    mx, my, mc = me // (Y * CORES), (me // CORES) % Y, me % CORES

    loads = [
        pltpu.make_async_copy(src, dst, in_sem.at[i])
        for i, (src, dst) in enumerate(
            [(ids_hbm, ids), (down_hbm, down), (up_hbm, up), (tok_hbm, tok), (cot_hbm, dy), (w_hbm, w)]
        )
    ]
    for load in loads:
        load.start()

    def group_peer(o):
        return ((mx + o[0]) % X) * (Y * CORES) + ((my + o[1]) % Y) * CORES + (mc + o[2]) % CORES

    barrier = pltpu.get_barrier_semaphore()
    for o in GREETINGS:
        to = (me, (col + o) % Z) if isinstance(o, int) else (group_peer(o), col)
        pl.semaphore_signal(barrier, inc=1, device_id=to, device_id_type=MESH)

    loads[0].wait()
    pairs = 2 * GROUPS
    at = lax.broadcasted_iota(jnp.int32, (pairs, GROUPS), 0) // 2
    lane = lax.broadcasted_iota(jnp.int32, (pairs, GROUPS), 1)
    own = jnp.sum(jnp.where(at == lane, ids[...].astype(F32), 0.0), axis=1, keepdims=True)
    row = lax.broadcasted_iota(jnp.int32, (pairs, adapters), 0)
    hit = lax.broadcasted_iota(jnp.int32, (pairs, adapters), 1).astype(F32) == own
    for h in range(2):
        pick[:, h * adapters:(h + 1) * adapters] = jnp.where(hit & (row % 2 == h), 1.0, 0.0).astype(BF16)
    even, odd = pick[:, :adapters], pick[:, adapters:]

    loads[1].wait()
    down_rows = nt(even, down[:LANES]) + nt(odd, down[LANES:])
    send1[0] = down_rows.astype(BF16).reshape(GROUPS, 2, LANES)
    loads[2].wait()
    up_wide = up[...].astype(F32)
    up_rows = nt(even, up_wide[:, 0, :].astype(BF16)) + nt(odd, up_wide[:, 1, :].astype(BF16))
    pad = jnp.zeros((pairs, LANES - rank), F32)
    send1[1] = jnp.concatenate([up_rows, pad], axis=1).astype(BF16).reshape(GROUPS, 2, LANES)

    pl.semaphore_wait(barrier, len(OFFSETS) + Z - 1)

    def exchange(src, dst, send_sem, recv_sem, local_sem):
        for o in OFFSETS:
            peer = group_peer(o)
            pltpu.make_async_remote_copy(
                src.at[:, peer], dst.at[:, me], send_sem, recv_sem,
                device_id=(peer, col), device_id_type=MESH,
            ).start()
        local = pltpu.make_async_copy(src.at[:, me], dst.at[:, me], local_sem)
        local.start()
        every = pltpu.make_async_remote_copy(
            src.at[:, 0:GROUPS - 1], dst.at[:, 0:GROUPS - 1], send_sem, recv_sem,
            device_id=(me, (col + 1) % Z), device_id_type=MESH,
        )
        return local, every

    def frozen_part(i):
        to = (col + i) % Z
        start = pl.multiple_of(to * cols, cols)
        return to, nn(tok[...], w[:, pl.ds(start, cols)])

    def send_chunk(i):
        to, value = frozen_part(i)
        chunk[i] = value.astype(BF16)
        pltpu.make_async_remote_copy(
            chunk.at[i], chunks.at[col], c_send, c_recv, device_id=(me, to), device_id_type=MESH
        ).start()

    loads[3].wait()
    loads[5].wait()
    local1, every1 = exchange(send1, recv1, a_send, a_recv, own_sem.at[0])

    for i in NEAR:
        send_chunk(i)

    i0 = lax.broadcasted_iota(jnp.int32, (LANES, LANES), 0)
    i1 = lax.broadcasted_iota(jnp.int32, (LANES, LANES), 1)
    order = jnp.where(i1 == (i0 % 32) * 4 + i0 // 32, 1.0, 0.0).astype(BF16)
    order_t = jnp.where(i0 == (i1 % 32) * 4 + i1 // 32, 1.0, 0.0).astype(BF16)
    blocks = features // LANES
    for k in range(blocks):
        span = slice(k * LANES, (k + 1) * LANES)
        tok_perm[:, span] = nt(tok[:, span], order).astype(BF16)
        turned = nt(order, tok[:, span]).astype(BF16)
        for j in range(4):
            tok_cols[k * 32:(k + 1) * 32, j * n:(j + 1) * n] = turned[j * 32:(j + 1) * 32]

    loads[4].wait()
    live = lax.broadcasted_iota(jnp.int32, (n, 1), 0) < rows_ref[0]
    mask = jnp.where(live, 1.0, 0.0)
    dy[...] = dy[...] * mask.astype(BF16)
    mine = pl.multiple_of(col * cols, cols)
    dy_cols[...] = dy[:, pl.ds(mine, cols)]
    dy_cols_t[...] = dy_cols[...].T
    frozen[...] = frozen_part(0)[1]

    local1.wait()
    every1.wait_recv()
    a_mat = recv1[0].reshape(pairs, LANES)
    b_mat = recv1[1].reshape(pairs, LANES)[:, :rank]
    a_tall = jnp.concatenate(
        [a_mat[k * 32:(k + 1) * 32, j * rank:(j + 1) * rank] for k in range(blocks) for j in range(4)], axis=0
    )
    sums = jnp.concatenate([nn(tok_perm[...], a_tall), nn(dy_cols[...], b_mat)], axis=1)
    half = n // 2
    part[...] = jnp.concatenate([sums[:half], sums[half:]], axis=1).astype(BF16)
    for i in range(Z - 1):
        to = i + (i - col + Z) // Z
        pltpu.make_async_remote_copy(
            part, parts.at[col], p_send, p_recv, device_id=(me, to), device_id_type=MESH
        ).start()
    parts[col] = part[...]

    for i in FAR:
        send_chunk(i)
    for k in range(blocks):
        span = slice(k * LANES, (k + 1) * LANES)
        m_down[span] = nn(order_t, a_tall[span]).astype(BF16)
    wide = 256
    for k in range(features // wide):
        back[:, k * wide:(k + 1) * wide] = nt(dy[...], w[k * wide:(k + 1) * wide, :])

    every_part = pltpu.make_async_remote_copy(
        parts.at[0:Z - 1], parts.at[0:Z - 1], p_send, p_recv,
        device_id=(me, (col + 1) % Z), device_id_type=MESH,
    )
    every_part.wait_recv()
    total = parts[0].astype(F32)
    for i in range(1, Z):
        total = total + parts[i].astype(F32)
    total = total.astype(BF16)
    act = jnp.concatenate([total[:, :rank], total[:, 2 * rank:3 * rank]], axis=0)
    grad = jnp.concatenate([total[:, rank:2 * rank], total[:, 3 * rank:]], axis=0)

    grad4 = jnp.concatenate([grad] * 4, axis=1)
    place = lax.broadcasted_iota(jnp.int32, (n, LANES), 1) // rank
    spread = jnp.concatenate(
        [jnp.where(place == j, grad4, jnp.zeros_like(grad4)) for j in range(4)], axis=0
    )
    send2[0] = nn(tok_cols[...], spread).astype(BF16).reshape(GROUPS, 2, LANES)
    up_term = nn(dy_cols_t[...], act)
    send2[1] = jnp.concatenate([up_term, pad], axis=1).astype(BF16).reshape(GROUPS, 2, LANES)
    local2, every2 = exchange(send2, recv2, g_send, g_recv, own_sem.at[1])

    tg[...] = (back[...] + nt(grad, m_down[...])).astype(BF16)
    every_chunk = pltpu.make_async_remote_copy(
        chunk.at[1:Z], chunks.at[0:Z - 1], c_send, c_recv,
        device_id=(me, (col + 1) % Z), device_id_type=MESH,
    )
    every_chunk.wait_recv()
    chunks[col] = jnp.zeros((n, cols), BF16)
    kv_sum = frozen[...] + nt(act, b_mat)
    for i in range(Z):
        kv_sum = kv_sum + chunks[i].astype(F32)
    kv[...] = (kv_sum * mask).astype(BF16)
    every1.wait_send()
    every_part.wait_send()
    every_chunk.wait_send()

    local2.wait()
    every2.wait_recv()
    every2.wait_send()


def finish(kv, tg, recv2, pick, kv_hbm, tg_hbm, gd_hbm, gu_hbm, gd, gu, sem):
    early = [
        pltpu.make_async_copy(src, dst, sem.at[i]) for i, (src, dst) in enumerate([(kv, kv_hbm), (tg, tg_hbm)])
    ]
    for copy in early:
        copy.start()
    pairs, adapters = pick.shape[0], pick.shape[1] // 2
    rank = gu.shape[0]
    terms = jnp.concatenate(
        [recv2[0].reshape(pairs, LANES).T, recv2[1].reshape(pairs, LANES).T[:rank]], axis=0
    )
    late = []
    for h in range(2):
        sums = nn(terms, pick[:, h * adapters:(h + 1) * adapters])
        rows = pl.ds(h * LANES, LANES)
        gd[rows] = sums[:LANES]
        late.append(pltpu.make_async_copy(gd.at[rows], gd_hbm.at[rows], sem.at[2 + h]))
        late[-1].start()
        gu[:, h, :] = sums[LANES:]
    late.append(pltpu.make_async_copy(gu, gu_hbm, sem.at[4]))
    late[-1].start()
    for copy in early + late:
        copy.wait()


def shards(tokens, kv_weight, adapter_down, adapter_up, cotangent, block_adapter, block_rows):
    n, features = tokens.shape
    kv_width = kv_weight.shape[1]
    adapters, _, slice_rows, rank = adapter_down.shape
    slice_cols = adapter_up.shape[3]
    cols = kv_width // Z
    down_table = adapter_down.transpose(1, 2, 3, 0).reshape(slice_rows * rank, adapters)
    up_table = adapter_up.transpose(2, 1, 3, 0).reshape(rank, slice_cols, adapters)
    ids = block_adapter.reshape(1, GROUPS)
    operands = [
        pltpu.with_memory_space_constraint(v, pltpu.HBM)
        for v in (tokens, kv_weight, down_table, up_table, cotangent, ids)
    ]
    pairs = 2 * GROUPS
    vmem, dma = pltpu.VMEM, pltpu.SemaphoreType.DMA
    hbm_spec = pl.BlockSpec(memory_space=pltpu.HBM)
    vmem_spec = pl.BlockSpec(memory_space=pltpu.VMEM)
    kv_shape = jax.ShapeDtypeStruct((n, cols), BF16)
    tg_shape = jax.ShapeDtypeStruct((n, features), BF16)
    kv, tg, recv2, pick = pl.pallas_call(
        kernel,
        out_shape=[
            kv_shape,
            tg_shape,
            jax.ShapeDtypeStruct((2, GROUPS, 2, LANES), BF16),
            jax.ShapeDtypeStruct((pairs, 2 * adapters), BF16),
        ],
        in_specs=[pl.BlockSpec(memory_space=pltpu.SMEM)] + [hbm_spec] * 6,
        out_specs=[vmem_spec] * 4,
        scratch_shapes=[
            vmem((n, features), BF16),
            vmem((features, kv_width), BF16),
            vmem((slice_rows * rank, adapters), BF16),
            vmem((rank, slice_cols, adapters), BF16),
            vmem((n, kv_width), BF16),
            vmem((1, GROUPS), jnp.int32),
            vmem((2, GROUPS, 2, LANES), BF16),
            vmem((2, GROUPS, 2, LANES), BF16),
            vmem((2, GROUPS, 2, LANES), BF16),
            vmem((n // 2, 4 * rank), BF16),
            vmem((Z, n // 2, 4 * rank), BF16),
            vmem((Z, n, cols), BF16),
            vmem((Z, n, cols), BF16),
            vmem((n, features), BF16),
            vmem((pairs, 4 * n), BF16),
            vmem((n, cols), BF16),
            vmem((cols, n), BF16),
            vmem((n, cols), F32),
            vmem((n, features), F32),
            vmem((features, rank), BF16),
            dma((6,)),
            dma((2,)),
            dma, dma, dma, dma, dma, dma, dma, dma,
        ],
        compiler_params=pltpu.CompilerParams(
            collective_id=0, has_side_effects=True, vmem_limit_bytes=40 << 20
        ),
        name="fused",
    )(block_rows, *operands)
    gd_shape = jax.ShapeDtypeStruct((slice_rows * rank, adapters), F32)
    gu_shape = jax.ShapeDtypeStruct((rank, slice_cols, adapters), F32)
    kv, tg, gd, gu = pl.pallas_call(
        finish,
        out_shape=[kv_shape, tg_shape, gd_shape, gu_shape],
        in_specs=[vmem_spec] * 4,
        out_specs=[hbm_spec] * 4,
        scratch_shapes=[vmem(gd_shape.shape, F32), vmem(gu_shape.shape, F32), dma((5,))],
        compiler_params=pltpu.CompilerParams(vmem_limit_bytes=16 << 20),
        name="finish",
    )(kv, tg, recv2, pick)
    grad_down = gd.reshape(1, slice_rows, rank, adapters).transpose(3, 0, 1, 2)
    grad_up = gu.reshape(1, rank, slice_cols, adapters).transpose(3, 1, 0, 2)
    return kv, tg, grad_down, grad_up


def solution(mesh):
    return jax.shard_map(
        shards,
        mesh=mesh,
        in_specs=(
            P("dp", "tensor"),
            P("tensor", None),
            P(None, "tensor", "dp", None),
            P(None, None, "tensor", "dp"),
            P("dp", None),
            P(),
            P("dp"),
        ),
        out_specs=(
            P("dp", "tensor"),
            P("dp", "tensor"),
            P(None, "tensor", "dp", None),
            P(None, None, "tensor", "dp"),
        ),
        check_vma=False,
    )
```

```python
import jax
import jax.numpy as jnp
from jax import lax
from jax.experimental import pallas as pl
from jax.experimental.pallas import tpu as pltpu
from jax.sharding import PartitionSpec as P

MESH = pl.DeviceIdType.MESH
BF16 = jnp.bfloat16
F32 = jnp.float32
X, Y, CORES, Z = 8, 8, 2, 8
GROUPS = X * Y * CORES
LANES = 128
STEPS = 3


def ring(step, size):
    return min(step, size - step)


OFFSETS = sorted(
    [(x, y, c) for x in range(X) for y in range(Y) for c in range(CORES) if (x, y, c) != (0, 0, 0)],
    key=lambda o: -(ring(o[0], X) + ring(o[1], Y)),
)
GREETINGS = sorted(
    OFFSETS + list(range(1, Z)),
    key=lambda o: -ring(o, Z) if isinstance(o, int) else -(ring(o[0], X) + ring(o[1], Y)),
)


def nn(a, b):
    return lax.dot_general(a, b, (((1,), (0,)), ((), ())), preferred_element_type=F32)


def nt(a, b):
    return lax.dot_general(a, b, (((1,), (1,)), ((), ())), preferred_element_type=F32)


def kernel(
    rows_ref, tok_hbm, w_hbm, down_hbm, up_hbm, cot_hbm, ids_hbm,
    kv, tg, recv2, pick,
    tok, w, down, up, dy, ids,
    send1, recv1, send2, part, parts, down_out, down_in, up_out, up_in, across_out, across_in,
    tok_perm, tok_cols, dy_cols, dy_cols_t, frozen, back, m_down,
    in_sem, own_sem, a_send, a_recv, p_send, p_recv, g_send, g_recv, d_send, d_recv, u_send, u_recv, x_send, x_recv,
):
    n, features = tok.shape
    rank = 32
    cols = kv.shape[1]
    adapters = down.shape[1]
    me = lax.axis_index("dp")
    col = lax.axis_index("tensor")
    mx, my, mc = me // (Y * CORES), (me // CORES) % Y, me % CORES

    loads = [
        pltpu.make_async_copy(src, dst, in_sem.at[i])
        for i, (src, dst) in enumerate(
            [(ids_hbm, ids), (down_hbm, down), (up_hbm, up), (tok_hbm, tok), (cot_hbm, dy), (w_hbm, w)]
        )
    ]
    for load in loads:
        load.start()

    def group_peer(o):
        return ((mx + o[0]) % X) * (Y * CORES) + ((my + o[1]) % Y) * CORES + (mc + o[2]) % CORES

    barrier = pltpu.get_barrier_semaphore()
    for o in GREETINGS:
        to = (me, (col + o) % Z) if isinstance(o, int) else (group_peer(o), col)
        pl.semaphore_signal(barrier, inc=1, device_id=to, device_id_type=MESH)

    loads[0].wait()
    pairs = 2 * GROUPS
    at = lax.broadcasted_iota(jnp.int32, (pairs, GROUPS), 0) // 2
    lane = lax.broadcasted_iota(jnp.int32, (pairs, GROUPS), 1)
    own = jnp.sum(jnp.where(at == lane, ids[...].astype(F32), 0.0), axis=1, keepdims=True)
    row = lax.broadcasted_iota(jnp.int32, (pairs, adapters), 0)
    hit = lax.broadcasted_iota(jnp.int32, (pairs, adapters), 1).astype(F32) == own
    for h in range(2):
        pick[:, h * adapters:(h + 1) * adapters] = jnp.where(hit & (row % 2 == h), 1.0, 0.0).astype(BF16)
    even, odd = pick[:, :adapters], pick[:, adapters:]

    loads[1].wait()
    down_rows = nt(even, down[:LANES]) + nt(odd, down[LANES:])
    send1[0] = down_rows.astype(BF16).reshape(GROUPS, 2, LANES)
    loads[2].wait()
    up_wide = up[...].astype(F32)
    up_rows = nt(even, up_wide[:, 0, :].astype(BF16)) + nt(odd, up_wide[:, 1, :].astype(BF16))
    pad = jnp.zeros((pairs, LANES - rank), F32)
    send1[1] = jnp.concatenate([up_rows, pad], axis=1).astype(BF16).reshape(GROUPS, 2, LANES)

    pl.semaphore_wait(barrier, len(OFFSETS) + Z - 1)

    def exchange(src, dst, send_sem, recv_sem, local_sem):
        for o in OFFSETS:
            peer = group_peer(o)
            pltpu.make_async_remote_copy(
                src.at[:, peer], dst.at[:, me], send_sem, recv_sem,
                device_id=(peer, col), device_id_type=MESH,
            ).start()
        local = pltpu.make_async_copy(src.at[:, me], dst.at[:, me], local_sem)
        local.start()
        every = pltpu.make_async_remote_copy(
            src.at[:, 0:GROUPS - 1], dst.at[:, 0:GROUPS - 1], send_sem, recv_sem,
            device_id=(me, (col + 1) % Z), device_id_type=MESH,
        )
        return local, every

    def frozen_part(i):
        start = pl.multiple_of((col + i) % Z * cols, cols)
        return nn(tok[...], w[:, pl.ds(start, cols)])

    def down_copy(s):
        return pltpu.make_async_remote_copy(
            down_out.at[s], down_in.at[s], d_send.at[s], d_recv.at[s],
            device_id=(me, (col + Z - 1) % Z), device_id_type=MESH,
        )

    def up_copy(s):
        return pltpu.make_async_remote_copy(
            up_out.at[s], up_in.at[s], u_send.at[s], u_recv.at[s],
            device_id=(me, (col + 1) % Z), device_id_type=MESH,
        )

    def across_copy():
        return pltpu.make_async_remote_copy(
            across_out, across_in, x_send, x_recv, device_id=(me, (col + Z // 2) % Z), device_id_type=MESH
        )

    def ring_step(s):
        total = frozen[Z - STEPS + s]
        if s:
            down_copy(s - 1).wait_recv()
            total = total + down_in[s - 1].astype(F32)
        down_out[s] = total.astype(BF16)
        down_copy(s).start()
        total = frozen[STEPS - s]
        if s:
            up_copy(s - 1).wait_recv()
            total = total + up_in[s - 1].astype(F32)
        up_out[s] = total.astype(BF16)
        up_copy(s).start()

    local1, every1 = exchange(send1, recv1, a_send, a_recv, own_sem.at[0])

    loads[3].wait()
    loads[5].wait()
    for i in (5, 3):
        frozen[i] = frozen_part(i)
    ring_step(0)
    across_out[...] = frozen_part(4).astype(BF16)
    across_copy().start()
    for i in (2, 6, 1, 7, 0):
        frozen[i] = frozen_part(i)

    i0 = lax.broadcasted_iota(jnp.int32, (LANES, LANES), 0)
    i1 = lax.broadcasted_iota(jnp.int32, (LANES, LANES), 1)
    order = jnp.where(i1 == (i0 % 32) * 4 + i0 // 32, 1.0, 0.0).astype(BF16)
    order_t = jnp.where(i0 == (i1 % 32) * 4 + i1 // 32, 1.0, 0.0).astype(BF16)
    blocks = features // LANES
    for k in range(blocks):
        span = slice(k * LANES, (k + 1) * LANES)
        tok_perm[:, span] = nt(tok[:, span], order).astype(BF16)
        turned = nt(order, tok[:, span]).astype(BF16)
        for j in range(4):
            tok_cols[k * 32:(k + 1) * 32, j * n:(j + 1) * n] = turned[j * 32:(j + 1) * 32]

    loads[4].wait()
    live = lax.broadcasted_iota(jnp.int32, (n, 1), 0) < rows_ref[0]
    mask = jnp.where(live, 1.0, 0.0)
    dy[...] = dy[...] * mask.astype(BF16)
    mine = pl.multiple_of(col * cols, cols)
    dy_cols[...] = dy[:, pl.ds(mine, cols)]
    dy_cols_t[...] = dy_cols[...].T

    local1.wait()
    every1.wait_recv()
    a_mat = recv1[0].reshape(pairs, LANES)
    b_mat = recv1[1].reshape(pairs, LANES)[:, :rank]
    a_tall = jnp.concatenate(
        [a_mat[k * 32:(k + 1) * 32, j * rank:(j + 1) * rank] for k in range(blocks) for j in range(4)], axis=0
    )
    sums = jnp.concatenate([nn(tok_perm[...], a_tall), nn(dy_cols[...], b_mat)], axis=1)
    half = n // 2
    part[...] = jnp.concatenate([sums[:half], sums[half:]], axis=1).astype(BF16)
    for i in range(Z - 1):
        to = i + (i - col + Z) // Z
        pltpu.make_async_remote_copy(
            part, parts.at[col], p_send, p_recv, device_id=(me, to), device_id_type=MESH
        ).start()
    parts[col] = part[...]

    ring_step(1)
    for k in range(blocks):
        span = slice(k * LANES, (k + 1) * LANES)
        m_down[span] = nn(order_t, a_tall[span]).astype(BF16)
    wide = 256
    for k in range(features // wide):
        back[:, k * wide:(k + 1) * wide] = nt(dy[...], w[k * wide:(k + 1) * wide, :])

    every_part = pltpu.make_async_remote_copy(
        parts.at[0:Z - 1], parts.at[0:Z - 1], p_send, p_recv,
        device_id=(me, (col + 1) % Z), device_id_type=MESH,
    )
    every_part.wait_recv()
    total = parts[0].astype(F32)
    for i in range(1, Z):
        total = total + parts[i].astype(F32)
    total = total.astype(BF16)
    act = jnp.concatenate([total[:, :rank], total[:, 2 * rank:3 * rank]], axis=0)
    grad = jnp.concatenate([total[:, rank:2 * rank], total[:, 3 * rank:]], axis=0)

    grad4 = jnp.concatenate([grad] * 4, axis=1)
    place = lax.broadcasted_iota(jnp.int32, (n, LANES), 1) // rank
    spread = jnp.concatenate(
        [jnp.where(place == j, grad4, jnp.zeros_like(grad4)) for j in range(4)], axis=0
    )
    send2[0] = nn(tok_cols[...], spread).astype(BF16).reshape(GROUPS, 2, LANES)
    up_term = nn(dy_cols_t[...], act)
    send2[1] = jnp.concatenate([up_term, pad], axis=1).astype(BF16).reshape(GROUPS, 2, LANES)
    local2, every2 = exchange(send2, recv2, g_send, g_recv, own_sem.at[1])

    ring_step(2)
    tg[...] = (back[...] + nt(grad, m_down[...])).astype(BF16)
    kv_sum = frozen[0] + nt(act, b_mat)
    up_copy(STEPS - 1).wait_recv()
    down_copy(STEPS - 1).wait_recv()
    across_copy().wait_recv()
    kv_sum = kv_sum + up_in[STEPS - 1].astype(F32) + down_in[STEPS - 1].astype(F32) + across_in[...].astype(F32)
    kv[...] = (kv_sum * mask).astype(BF16)
    every1.wait_send()
    every_part.wait_send()
    for s in range(STEPS):
        down_copy(s).wait_send()
        up_copy(s).wait_send()
    across_copy().wait_send()

    local2.wait()
    every2.wait_recv()
    every2.wait_send()


def finish(kv, tg, recv2, pick, kv_hbm, tg_hbm, gd_hbm, gu_hbm, gd, gu, sem):
    early = [
        pltpu.make_async_copy(src, dst, sem.at[i]) for i, (src, dst) in enumerate([(kv, kv_hbm), (tg, tg_hbm)])
    ]
    for copy in early:
        copy.start()
    pairs, adapters = pick.shape[0], pick.shape[1] // 2
    rank = gu.shape[0]
    terms = jnp.concatenate(
        [recv2[0].reshape(pairs, LANES).T, recv2[1].reshape(pairs, LANES).T[:rank]], axis=0
    )
    late = []
    for h in range(2):
        sums = nn(terms, pick[:, h * adapters:(h + 1) * adapters])
        rows = pl.ds(h * LANES, LANES)
        gd[rows] = sums[:LANES]
        late.append(pltpu.make_async_copy(gd.at[rows], gd_hbm.at[rows], sem.at[2 + h]))
        late[-1].start()
        gu[:, h, :] = sums[LANES:]
    late.append(pltpu.make_async_copy(gu, gu_hbm, sem.at[4]))
    late[-1].start()
    for copy in early + late:
        copy.wait()


def shards(tokens, kv_weight, adapter_down, adapter_up, cotangent, block_adapter, block_rows):
    n, features = tokens.shape
    kv_width = kv_weight.shape[1]
    adapters, _, slice_rows, rank = adapter_down.shape
    slice_cols = adapter_up.shape[3]
    cols = kv_width // Z
    down_table = adapter_down.transpose(1, 2, 3, 0).reshape(slice_rows * rank, adapters)
    up_table = adapter_up.transpose(2, 1, 3, 0).reshape(rank, slice_cols, adapters)
    ids = block_adapter.reshape(1, GROUPS)
    operands = [
        pltpu.with_memory_space_constraint(v, pltpu.HBM)
        for v in (tokens, kv_weight, down_table, up_table, cotangent, ids)
    ]
    pairs = 2 * GROUPS
    vmem, dma = pltpu.VMEM, pltpu.SemaphoreType.DMA
    hbm_spec = pl.BlockSpec(memory_space=pltpu.HBM)
    vmem_spec = pl.BlockSpec(memory_space=pltpu.VMEM)
    kv_shape = jax.ShapeDtypeStruct((n, cols), BF16)
    tg_shape = jax.ShapeDtypeStruct((n, features), BF16)
    kv, tg, recv2, pick = pl.pallas_call(
        kernel,
        out_shape=[
            kv_shape,
            tg_shape,
            jax.ShapeDtypeStruct((2, GROUPS, 2, LANES), BF16),
            jax.ShapeDtypeStruct((pairs, 2 * adapters), BF16),
        ],
        in_specs=[pl.BlockSpec(memory_space=pltpu.SMEM)] + [hbm_spec] * 6,
        out_specs=[vmem_spec] * 4,
        scratch_shapes=[
            vmem((n, features), BF16),
            vmem((features, kv_width), BF16),
            vmem((slice_rows * rank, adapters), BF16),
            vmem((rank, slice_cols, adapters), BF16),
            vmem((n, kv_width), BF16),
            vmem((1, GROUPS), jnp.int32),
            vmem((2, GROUPS, 2, LANES), BF16),
            vmem((2, GROUPS, 2, LANES), BF16),
            vmem((2, GROUPS, 2, LANES), BF16),
            vmem((n // 2, 4 * rank), BF16),
            vmem((Z, n // 2, 4 * rank), BF16),
            vmem((STEPS, n, cols), BF16),
            vmem((STEPS, n, cols), BF16),
            vmem((STEPS, n, cols), BF16),
            vmem((STEPS, n, cols), BF16),
            vmem((n, cols), BF16),
            vmem((n, cols), BF16),
            vmem((n, features), BF16),
            vmem((pairs, 4 * n), BF16),
            vmem((n, cols), BF16),
            vmem((cols, n), BF16),
            vmem((Z, n, cols), F32),
            vmem((n, features), F32),
            vmem((features, rank), BF16),
            dma((6,)),
            dma((2,)),
            dma, dma, dma, dma, dma, dma,
            dma((STEPS,)), dma((STEPS,)), dma((STEPS,)), dma((STEPS,)), dma, dma,
        ],
        compiler_params=pltpu.CompilerParams(
            collective_id=0, has_side_effects=True, vmem_limit_bytes=40 << 20
        ),
        name="fused",
    )(block_rows, *operands)
    gd_shape = jax.ShapeDtypeStruct((slice_rows * rank, adapters), F32)
    gu_shape = jax.ShapeDtypeStruct((rank, slice_cols, adapters), F32)
    kv, tg, gd, gu = pl.pallas_call(
        finish,
        out_shape=[kv_shape, tg_shape, gd_shape, gu_shape],
        in_specs=[vmem_spec] * 4,
        out_specs=[hbm_spec] * 4,
        scratch_shapes=[vmem(gd_shape.shape, F32), vmem(gu_shape.shape, F32), dma((5,))],
        compiler_params=pltpu.CompilerParams(vmem_limit_bytes=16 << 20),
        name="finish",
    )(kv, tg, recv2, pick)
    grad_down = gd.reshape(1, slice_rows, rank, adapters).transpose(3, 0, 1, 2)
    grad_up = gu.reshape(1, rank, slice_cols, adapters).transpose(3, 1, 0, 2)
    return kv, tg, grad_down, grad_up


def solution(mesh):
    return jax.shard_map(
        shards,
        mesh=mesh,
        in_specs=(
            P("dp", "tensor"),
            P("tensor", None),
            P(None, "tensor", "dp", None),
            P(None, None, "tensor", "dp"),
            P("dp", None),
            P(),
            P("dp"),
        ),
        out_specs=(
            P("dp", "tensor"),
            P("dp", "tensor"),
            P(None, "tensor", "dp", None),
            P(None, None, "tensor", "dp"),
        ),
        check_vma=False,
    )
```
